512 devices in a mesh: chan: 8 (over x, y_lo), ctx: 64 (over y_hi, z, core).
Axes of the slice: x: 4, y: 8 (y_hi: 4, y_lo: 2; y = y_hi * 2 + y_lo), z: 8, core: 2. Of those that a mesh axis runs over, the one named last changes fastest.
Arguments:
- value: bfloat16 [2, 8192, 2048], P(None, 'ctx', 'chan'), may hold values from -6 to 6
- gate_in: bfloat16 [2, 8192, 2048], P(None, 'ctx', 'chan'), may hold values from -6 to 6
- gate_out: bfloat16 [2, 8192, 2048], P(None, 'ctx', 'chan'), may hold values from -6 to 6
- filters: float32 [384, 2048], P(None, 'chan'), may hold values from -0.3125 to 0.3125
- skip: float32 [2048], P('chan'), may hold values from -5 to 5
- proj: bfloat16 [2048, 2048], P(('chan', 'ctx')), may hold values from -0.125 to 0.125
- taps: float32 [128, 2048], P(None, 'chan'), may hold values from -0.5 to 0.5
Outputs:
- result: bfloat16 [2, 8192, 2048], P(None, 'ctx', 'chan')
The draws below stay inside these ranges and needn't reach their ends.
All inputs are finite; a program needn't handle non-finite values.
Results may differ from the reference program's by a relative error of at most 0.0057.
Values may be sent and summed in bfloat16 or wider, within the bound.
No kernel may reach another device: no remote copies, remote signals or barrier semaphores. Data moves between devices by JAX's collectives and lax.ppermute only.
A program may use at most 64 MiB of HBM per device.

```python
import jax
import jax.numpy as jnp
from jax import lax

D = 2048
BATCH = 2
SHORT = 128
LENGTH = 8192
LAGS = 384
N_CHAN = 8


def level_of(rng, dims, cuts, least, largest):
    def one(dim, shards_of):
        heights = jax.random.uniform(jax.random.fold_in(jax.random.fold_in(rng, 6), dim), (shards_of,), jnp.float32, least / len(cuts), largest / len(cuts))
        return jnp.repeat(jnp.exp(heights), dims[dim] // shards_of).reshape((-1,) + (1,) * (len(dims) - dim - 1))

    level = one(*cuts[0])
    for cut in cuts[1:]:
        level = level * one(*cut)
    return level


def normal_values(rng, shape, width, limit, cuts=(), dtype=jnp.bfloat16):
    drawn = width * jax.random.normal(rng, shape, jnp.float32)
    if cuts:
        drawn = drawn * level_of(rng, shape, cuts, -0.22, 0.18)
    return jnp.clip(drawn, -limit, limit).astype(dtype)


def setup_inputs(seed: int = 0) -> dict:
    key_list = jax.random.split(jax.random.key(seed), 8)
    value = normal_values(key_list[0], (BATCH, LENGTH, D), 1.0, 6.0, ((1, 64), (2, 8)))
    gate_in = normal_values(key_list[1], (BATCH, LENGTH, D), 1.0, 6.0, ((1, 64), (2, 8)))
    gate_out = normal_values(key_list[2], (BATCH, LENGTH, D), 1.0, 6.0, ((1, 64), (2, 8)))
    filters = normal_values(key_list[3], (LAGS, D), LAGS ** -0.5, 0.3125, ((1, 8),), jnp.float32)
    skip = normal_values(key_list[4], (D,), 1.0, 5.0, ((0, 8),), jnp.float32)
    proj = normal_values(key_list[5], (D, D), D ** -0.5, 0.125, ((0, 512),))
    taps = normal_values(key_list[6], (SHORT, D), SHORT ** -0.5, 0.5, ((1, 8),), jnp.float32)
    return {"value": value, "gate_in": gate_in, "gate_out": gate_out, "filters": filters, "skip": skip, "proj": proj, "taps": taps}


def causal_conv(signal, kernel):
    length_total = 2 * signal.shape[0]
    signal_spec = jnp.fft.rfft(signal, n=length_total, axis=0)
    kernel_spec = jnp.fft.rfft(kernel, n=length_total, axis=0)
    return jnp.fft.irfft(signal_spec * kernel_spec, n=length_total, axis=0)[: signal.shape[0]]


def one_sequence(value, gate_in, gate_out, filters, skip, proj, taps):
    group_width = D // N_CHAN
    value_wide = value.astype(jnp.float32)
    value_groups = value_wide.reshape(LENGTH, N_CHAN, group_width).transpose(1, 0, 2)
    filter_groups = filters.astype(jnp.float32).reshape(LAGS, N_CHAN, group_width).transpose(1, 0, 2)
    conv = lax.map(lambda pair: causal_conv(pair[0], pair[1]), (value_groups, filter_groups))
    conv = conv.transpose(1, 0, 2).reshape(LENGTH, D)
    mixed = (gate_in.astype(jnp.float32) * (conv + skip.astype(jnp.float32)[None, :] * value_wide)).astype(jnp.bfloat16)
    projected = jnp.dot(mixed, proj, preferred_element_type=jnp.float32).astype(jnp.bfloat16)
    proj_groups = projected.astype(jnp.float32).reshape(LENGTH, N_CHAN, group_width).transpose(1, 0, 2)
    tap_groups = taps.astype(jnp.float32).reshape(SHORT, N_CHAN, group_width).transpose(1, 0, 2)
    shorted = lax.map(lambda pair: causal_conv(pair[0], pair[1]), (proj_groups, tap_groups))
    shorted = shorted.transpose(1, 0, 2).reshape(LENGTH, D)
    return (gate_out.astype(jnp.float32) * shorted).astype(jnp.bfloat16)


def reference(value, gate_in, gate_out, filters, skip, proj, taps):
    return lax.map(lambda trio: one_sequence(trio[0], trio[1], trio[2], filters, skip, proj, taps), (value, gate_in, gate_out))
```

```python
import jax
import jax.numpy as jnp
import ml_dtypes
import numpy as np
from jax import lax
from jax.experimental import pallas as pl
from jax.experimental.pallas import tpu as pltpu
from jax.sharding import PartitionSpec as P

F32 = jnp.float32
BF16 = jnp.bfloat16
VMEM = pl.BlockSpec(memory_space=pltpu.VMEM)
SMEM = pl.BlockSpec(memory_space=pltpu.SMEM)


def split_table(table):
    high = table.astype(ml_dtypes.bfloat16)
    low = (table - high.astype(np.float64)).astype(ml_dtypes.bfloat16)
    return high, low


def odd_tables(period, block):
    half = period // 2
    turn = (2 * np.arange(half)[:, None] + 1) * np.arange(period)[None, :] % (2 * period)
    phase = np.pi * turn / period
    forward = np.concatenate([np.cos(phase), -np.sin(phase)], axis=0)
    inverse = forward[:, period - block :].T / half
    return split_table(forward), split_table(inverse)


def halves(value):
    high = value.astype(BF16)
    return high, (value - high.astype(F32)).astype(BF16)


def dot(left, right):
    return jnp.dot(left, right, preferred_element_type=F32)


def wide_dot(table_high, table_low, operand):
    high, low = halves(operand)
    return dot(table_high, high) + dot(table_high, low) + dot(table_low, high)


def exact_dot(table_high, table_low, operand):
    return dot(table_high, operand) + dot(table_low, operand)


def spectra_product(first, second):
    half = first.shape[0] // 2
    a_re, a_im, b_re, b_im = first[:half], first[half:], second[:half], second[half:]
    return jnp.concatenate([a_re * b_re - a_im * b_im, a_re * b_im + a_im * b_re], axis=0)


def filter_kernel(filters, taps, long_high, long_low, short_high, short_low, long_spec, short_spec):
    lags, count = filters.shape[0], taps.shape[0]
    long_spec[...] = wide_dot(long_high[:, :lags], long_low[:, :lags], filters[...])
    short_spec[...] = wide_dot(short_high[:, :count], short_low[:, :count], taps[...])


def mixed_kernel(
    core, third, second, first, value, gate, skip, spec, f_high, f_low, i_high, i_low, mixed, window
):
    batch, rows, channels = value.shape
    source = lax.broadcasted_iota(jnp.int32, (channels, channels), 0)
    place = lax.broadcasted_iota(jnp.int32, (channels, channels), 1)
    half = lax.bitwise_xor(lax.shift_right_logical(source, 2) & 1, core[0])
    target = half * (channels // 2) + lax.shift_right_logical(source, 3) * 4 + (source & 3)
    order = (target == place).astype(F32).astype(BF16)
    for b in range(batch):
        for part, ref in enumerate((third, second, first, value)):
            window[part * rows : (part + 1) * rows, :] = ref[b]
        spectrum = exact_dot(f_high[...], f_low[...], window[...])
        product = spectra_product(spectrum, spec[...])
        conv = wide_dot(i_high[...], i_low[...], product)
        own = value[b].astype(F32)
        result = (gate[b].astype(F32) * (conv + skip[...] * own)).astype(BF16)
        mixed[b * rows : (b + 1) * rows, :] = dot(result, order).astype(BF16)


def project_kernel(mixed, own, other, partial):
    half = own.shape[0]
    width = partial.shape[2]
    for group in range(partial.shape[0]):
        columns = slice(group * width, (group + 1) * width)
        partial[group] = (
            dot(mixed[:, :half], own[:, columns]) + dot(mixed[:, half:], other[:, columns])
        ).astype(BF16)


def sum_kernel(parts, total):
    value = parts[0].astype(F32)
    for group in range(1, parts.shape[0]):
        value = value + parts[group].astype(F32)
    total[...] = value.astype(BF16)


def output_kernel(rim, own, gate, spec, f_high, f_low, i_high, i_low, result, window):
    batch, rows, _ = gate.shape
    for b in range(batch):
        window[:rows, :] = rim[b * rows : (b + 1) * rows, :]
        window[rows:, :] = own[b * rows : (b + 1) * rows, :]
        spectrum = exact_dot(f_high[...], f_low[...], window[...])
        product = spectra_product(spectrum, spec[...])
        shorted = wide_dot(i_high[...], i_low[...], product)
        result[b] = (gate[b].astype(F32) * shorted).astype(BF16)


def call(kernel, outs, flops, scratch=()):
    def run(*args):
        many = isinstance(outs, (list, tuple))
        specs = [SMEM if a.dtype == jnp.int32 else VMEM for a in args]
        size = sum(a.size * a.dtype.itemsize for a in args)
        return pl.pallas_call(
            kernel,
            out_shape=outs,
            in_specs=specs,
            out_specs=[VMEM] * len(outs) if many else VMEM,
            scratch_shapes=list(scratch),
            compiler_params=pltpu.CompilerParams(vmem_limit_bytes=48 * 1024 * 1024),
            cost_estimate=pl.CostEstimate(flops=flops, bytes_accessed=size, transcendentals=0),
        )(*args)

    return run


def from_behind(value, steps):
    count = lax.axis_size("ctx")
    return lax.ppermute(value, "ctx", [(s, s + steps) for s in range(count - steps)])


def spread(value, groups):
    count = len(groups[0])
    copies = jnp.broadcast_to(value[None], (count,) + value.shape)
    return lax.all_to_all(copies, "ctx", 0, 0, axis_index_groups=groups, tiled=True)


def shape(dims, dtype):
    return jax.ShapeDtypeStruct(dims, dtype)


def per_device(value, gate_in, gate_out, filters, skip, proj, taps):
    batch, rows, channels = value.shape
    lags, count = filters.shape[0], taps.shape[0]
    period, short_period = lags + rows, count + rows
    (f_high, f_low), (i_high, i_low) = odd_tables(period, rows)
    (sf_high, sf_low), (si_high, si_low) = odd_tables(short_period, rows)

    along_z = [[y * 16 + z * 2 + c for z in range(8)] for y in range(4) for c in range(2)]
    along_y = [[y * 16 + z * 2 + c for y in range(4)] for z in range(8) for c in range(2)]
    lines = spread(proj, along_z).reshape(-1, proj.shape[1])
    first = from_behind(value, 1)
    second = from_behind(value, 2)
    third = from_behind(value, 3)
    plane = spread(lines, along_y).reshape(-1, proj.shape[1])
    other = lax.ppermute(plane, "ctx", [(s, s ^ 1) for s in range(lax.axis_size("ctx"))])
    core = (lax.axis_index("ctx") % 2).astype(jnp.int32).reshape(1)

    spec, short_spec = call(
        filter_kernel,
        (shape((period, channels), F32), shape((short_period, channels), F32)),
        3 * 2 * period * lags * channels,
    )(filters, taps, f_high, f_low, sf_high, sf_low)
    mixed = call(
        mixed_kernel,
        shape((batch * rows, channels), BF16),
        batch * 2 * period * period * channels * 3,
        [pltpu.VMEM((period, channels), BF16)],
    )(core, third, second, first, value, gate_in, skip[None], spec, f_high, f_low, i_high, i_low)
    groups = lax.axis_size("chan")
    partial = call(
        project_kernel,
        shape((groups, batch * rows, channels), BF16),
        2 * batch * rows * channels * channels * groups,
    )(mixed, plane, other)
    parts = lax.all_to_all(partial, "chan", 0, 0, tiled=True)
    projected = call(
        sum_kernel, shape((batch * rows, channels), BF16), batch * rows * channels * groups
    )(parts)
    rim = from_behind(projected, 1)
    return call(
        output_kernel,
        shape((batch, rows, channels), BF16),
        batch * 2 * short_period * short_period * channels * 3,
        [pltpu.VMEM((short_period, channels), BF16)],
    )(rim, projected, gate_out, short_spec, sf_high, sf_low, si_high, si_low)


def solution(mesh):
    in_specs = (
        P(None, "ctx", "chan"),
        P(None, "ctx", "chan"),
        P(None, "ctx", "chan"),
        P(None, "chan"),
        P("chan"),
        P(("chan", "ctx"), None),
        P(None, "chan"),
    )
    out_specs = P(None, "ctx", "chan")
    return jax.shard_map(
        per_device, mesh=mesh, in_specs=in_specs, out_specs=out_specs, check_vma=False
    )
```

```python
import functools

import jax
import jax.numpy as jnp
import ml_dtypes
import numpy as np
from jax import lax
from jax.experimental import pallas as pl
from jax.experimental.pallas import tpu as pltpu
from jax.sharding import PartitionSpec as P

F32 = jnp.float32
BF16 = jnp.bfloat16
VMEM = pl.BlockSpec(memory_space=pltpu.VMEM)
SMEM = pl.BlockSpec(memory_space=pltpu.SMEM)
HBM = pl.BlockSpec(memory_space=pltpu.HBM)


def split_table(table):
    high = table.astype(ml_dtypes.bfloat16)
    low = (table - high.astype(np.float64)).astype(ml_dtypes.bfloat16)
    return high, low


def odd_tables(period, block):
    half = period // 2
    turn = (2 * np.arange(half)[:, None] + 1) * np.arange(period)[None, :] % (2 * period)
    phase = np.pi * turn / period
    forward = np.concatenate([np.cos(phase), -np.sin(phase)], axis=0)
    inverse = forward[:, period - block :].T / half
    return split_table(forward), split_table(inverse)


class Tables:
    def __init__(self, period, short_period, block):
        (f_high, f_low), (i_high, i_low) = odd_tables(period, block)
        (sf_high, sf_low), (si_high, si_low) = odd_tables(short_period, block)
        width = period
        self.places, rows, top = {}, [], 0
        for name, table in (("f_high", f_high), ("f_low", f_low), ("i_high", i_high), ("i_low", i_low)):
            self.places[name] = (slice(top, top + table.shape[0]), slice(0, width))
            rows.append(table)
            top += table.shape[0]
        for name, pair in (("sf", (sf_high, sf_low)), ("si", (si_high, si_low))):
            cols, height = pair[0].shape[1], pair[0].shape[0]
            self.places[name + "_high"] = (slice(top, top + height), slice(0, cols))
            self.places[name + "_low"] = (slice(top, top + height), slice(cols, 2 * cols))
            pad = np.zeros((height, width - 2 * cols), ml_dtypes.bfloat16)
            rows.append(np.concatenate([*pair, pad], axis=1))
            top += height
        self.packed = np.concatenate(rows, axis=0)

    def get(self, ref, name, first=None, last=None):
        rows, cols = self.places[name]
        start = cols.start + (first or 0)
        stop = cols.stop if last is None else cols.start + last
        return ref[rows, start:stop]


def halves(value):
    high = value.astype(BF16)
    return high, (value - high.astype(F32)).astype(BF16)


def dot(left, right):
    return jnp.dot(left, right, preferred_element_type=F32)


def wide_dot(table_high, table_low, operand):
    high, low = halves(operand)
    return dot(table_high, high) + dot(table_high, low) + dot(table_low, high)


def exact_dot(table_high, table_low, operand):
    return dot(table_high, operand) + dot(table_low, operand)


def spectra_product(first, second):
    half = first.shape[0] // 2
    a_re, a_im, b_re, b_im = first[:half], first[half:], second[:half], second[half:]
    return jnp.concatenate([a_re * b_re - a_im * b_im, a_re * b_im + a_im * b_re], axis=0)


def pieces_kernel(proj, pieces):
    width = pieces.shape[2] // 8
    for part in range(2):
        for group in range(8):
            start = (group * 2 + part) * width
            columns = proj[:, start : start + width]
            for z in range(pieces.shape[0] // 2):
                pieces[z * 2 + part, :, group * width : (group + 1) * width] = columns


def lines_kernel(lines, copies, flat):
    depth, width = lines.shape[1], lines.shape[2] // 8
    for source in range(lines.shape[0]):
        flat[source * depth : (source + 1) * depth, :] = lines[source].astype(F32)
    for low in range(2):
        for x in range(4):
            start = (x * 2 + low) * width
            columns = flat[:, start : start + width].astype(BF16)
            for high in range(4):
                copies[low * 4 + high, :, x * width : (x + 1) * width] = columns


def filter_kernel(
    tables, filters_hbm, skip_hbm, taps_hbm, packed_hbm, long_spec, short_spec, filters, skip, taps, packed, sems
):
    pairs = ((filters_hbm, filters), (skip_hbm, skip), (taps_hbm, taps), (packed_hbm, packed))
    copies = [
        pltpu.make_async_copy(source, target, sems.at[i]) for i, (source, target) in enumerate(pairs)
    ]
    for copy in copies:
        copy.start()
    for copy in copies:
        copy.wait()
    lags, count = filters.shape[0], taps.shape[0]
    newest = lax.broadcasted_iota(jnp.int32, filters.shape, 0) == 0
    with_skip = filters[...] + jnp.where(newest, skip[...], 0.0)
    get = functools.partial(tables.get, packed)
    long_spec[...] = wide_dot(get("f_high", 0, lags), get("f_low", 0, lags), with_skip)
    short_spec[...] = wide_dot(get("sf_high", 0, count), get("sf_low", 0, count), taps[...])


def near_kernel(tables, second, first, value, packed, near, window):
    batch, rows, _ = value.shape
    get = functools.partial(tables.get, packed)
    for b in range(batch):
        for part, ref in enumerate((second, first, value)):
            window[part * rows : (part + 1) * rows, :] = ref[b]
        near[b] = exact_dot(get("f_high", rows), get("f_low", rows), window[...])


def mixed_kernel(tables, third, near, gate, spec, packed, mixed):
    batch, rows, _ = gate.shape
    get = functools.partial(tables.get, packed)
    for b in range(batch):
        spectrum = near[b] + exact_dot(get("f_high", 0, rows), get("f_low", 0, rows), third[b])
        conv = wide_dot(get("i_high"), get("i_low"), spectra_product(spectrum, spec[...]))
        mixed[b * rows : (b + 1) * rows, :] = (gate[b].astype(F32) * conv).astype(BF16)


def project_kernel(place, mine, over_low, over_core, over_both, plane, partial):
    core, low = place[0], place[1]
    channels, width = mine.shape[1], partial.shape[2]
    near = plane[pl.ds(pl.multiple_of(low * channels, channels), channels), :]
    far = plane[pl.ds(pl.multiple_of((1 - low) * channels, channels), channels), :]
    for here, there, block in ((mine, over_low, core), (over_core, over_both, 1 - core)):
        total = dot(here[...], near) + dot(there[...], far)
        for x in range(partial.shape[0] // 2):
            partial[x * 2 + block] = total[:, x * width : (x + 1) * width].astype(BF16)


def sum_kernel(parts, total):
    cores, width = 2, parts.shape[2]
    for core in range(cores):
        value = parts[core].astype(F32)
        for x in range(1, parts.shape[0] // cores):
            value = value + parts[x * cores + core].astype(F32)
        total[:, core * width : (core + 1) * width] = value.astype(BF16)


def own_kernel(tables, own, packed, near):
    rows = own.shape[0] // near.shape[0]
    skipped = near.shape[1] - rows
    get = functools.partial(tables.get, packed)
    for b in range(near.shape[0]):
        block = own[b * rows : (b + 1) * rows, :]
        near[b] = exact_dot(get("sf_high", skipped), get("sf_low", skipped), block)


def output_kernel(tables, rim, near, gate, spec, packed, result):
    batch, rows, _ = gate.shape
    skipped = near.shape[1] - rows
    get = functools.partial(tables.get, packed)
    for b in range(batch):
        block = rim[b * rows : (b + 1) * rows, :]
        spectrum = near[b] + exact_dot(get("sf_high", 0, skipped), get("sf_low", 0, skipped), block)
        shorted = wide_dot(get("si_high"), get("si_low"), spectra_product(spectrum, spec[...]))
        result[b] = (gate[b].astype(F32) * shorted).astype(BF16)


def call(kernel, outs, flops, scratch=(), left=(), grant=48):
    def run(*args):
        many = isinstance(outs, (list, tuple))
        specs = [HBM if i in left else SMEM if a.dtype == jnp.int32 else VMEM for i, a in enumerate(args)]
        size = sum(a.size * a.dtype.itemsize for a in args)
        return pl.pallas_call(
            kernel,
            out_shape=outs,
            in_specs=specs,
            out_specs=[VMEM] * len(outs) if many else VMEM,
            scratch_shapes=list(scratch),
            compiler_params=pltpu.CompilerParams(vmem_limit_bytes=grant * 1024 * 1024),
            cost_estimate=pl.CostEstimate(flops=flops, bytes_accessed=size, transcendentals=0),
        )(*args)

    return run


def from_behind(value, steps):
    count = lax.axis_size("ctx")
    return lax.ppermute(value, "ctx", [(s, s + steps) for s in range(count - steps)])


def shape(dims, dtype):
    return jax.ShapeDtypeStruct(dims, dtype)


def after(value, *earlier):
    return lax.optimization_barrier((value,) + earlier)[0]


def per_device(value, gate_in, gate_out, filters, skip, proj, taps):
    batch, rows, channels = value.shape
    lags, count = filters.shape[0], taps.shape[0]
    period, short_period = lags + rows, count + rows
    tables = Tables(period, short_period, rows)
    packed = jnp.asarray(tables.packed)
    place = jnp.stack([lax.axis_index("ctx") % 2, lax.axis_index("chan") % 2]).astype(jnp.int32)
    depth, width = proj.shape
    wide = batch * rows
    part = channels // 2

    def device(x, low, high, z, core):
        return (x * 2 + low) * 64 + high * 16 + z * 2 + core

    def exchange(pieces, groups):
        return lax.all_to_all(
            pieces, ("chan", "ctx"), 0, 0, axis_index_groups=groups, tiled=True
        )

    xs, lows, highs, zs, cores = range(4), range(2), range(4), range(8), range(2)
    along_z = [
        [device(x, low, high, z, c) for z in zs for c in cores]
        for x in xs for low in lows for high in highs
    ]
    along_y = [
        [device(x, low, high, z, c) for low in lows for high in highs]
        for x in xs for z in zs for c in cores
    ]
    along_x = [
        [device(x, low, high, z, c) for x in xs for c in cores]
        for low in lows for high in highs for z in zs
    ]

    pieces = call(pieces_kernel, shape((16, depth, width // 2), BF16), 1000)(proj)
    lines = exchange(pieces, along_z)
    first = from_behind(value, 1)
    second = from_behind(value, 2)
    spec, short_spec = call(
        functools.partial(filter_kernel, tables),
        (shape((period, channels), F32), shape((short_period, channels), F32)),
        3 * 2 * period * lags * channels,
        [
            pltpu.VMEM(filters.shape, F32),
            pltpu.VMEM((1, channels), F32),
            pltpu.VMEM(taps.shape, F32),
            pltpu.VMEM(packed.shape, BF16),
            pltpu.SemaphoreType.DMA((4,)),
        ],
        (0, 1, 2, 3),
        60,
    )(filters, skip[None], taps, packed)
    third = from_behind(second, 1)
    lines = call(
        lines_kernel,
        shape((8, 16 * depth, width // 4), BF16),
        1000,
        [pltpu.VMEM((16 * depth, width // 2), F32)],
    )(after(lines, third))
    plane = exchange(lines, along_y).reshape(8 * 16 * depth, width // 4)
    near = call(
        functools.partial(near_kernel, tables),
        shape((batch, period, channels), F32),
        40 * batch * 2 * period * lags * channels,
        [pltpu.VMEM((lags, channels), BF16)],
    )(second, first, value, packed)
    mixed = call(
        functools.partial(mixed_kernel, tables),
        shape((wide, channels), BF16),
        20 * batch * 2 * period * rows * channels * 5,
    )(third, near, gate_in, spec, packed)

    def across(flip):
        pairs = [(d, d ^ flip) for d in range(lax.axis_size("chan") * lax.axis_size("ctx"))]
        return lax.ppermute(mixed, ("chan", "ctx"), pairs)

    over_low, over_core, over_both = across(64), across(1), across(65)
    partial = call(
        project_kernel, shape((8, wide, part), BF16), 2 * wide * 2 * channels * width
    )(place, mixed, over_low, over_core, over_both, plane)
    parts = exchange(partial, along_x)
    projected = call(sum_kernel, shape((wide, channels), BF16), wide * channels * 4)(parts)
    rim = from_behind(projected, 1)
    near = call(
        functools.partial(own_kernel, tables),
        shape((batch, short_period, channels), F32),
        2 * batch * 2 * short_period * rows * channels,
    )(projected, packed)
    return call(
        functools.partial(output_kernel, tables),
        shape((batch, rows, channels), BF16),
        batch * 2 * short_period * rows * channels * 5,
    )(rim, near, gate_out, short_spec, packed)


def solution(mesh):
    in_specs = (
        P(None, "ctx", "chan"),
        P(None, "ctx", "chan"),
        P(None, "ctx", "chan"),
        P(None, "chan"),
        P("chan"),
        P(("chan", "ctx"), None),
        P(None, "chan"),
    )
    out_specs = P(None, "ctx", "chan")
    return jax.shard_map(
        per_device, mesh=mesh, in_specs=in_specs, out_specs=out_specs, check_vma=False
    )
```

```python
import functools

import jax
import jax.numpy as jnp
import ml_dtypes
import numpy as np
from jax import lax
from jax.experimental import pallas as pl
from jax.experimental.pallas import tpu as pltpu
from jax.sharding import PartitionSpec as P

F32 = jnp.float32
BF16 = jnp.bfloat16
VMEM = pl.BlockSpec(memory_space=pltpu.VMEM)
SMEM = pl.BlockSpec(memory_space=pltpu.SMEM)
HBM = pl.BlockSpec(memory_space=pltpu.HBM)


def split_table(table):
    high = table.astype(ml_dtypes.bfloat16)
    low = (table - high.astype(np.float64)).astype(ml_dtypes.bfloat16)
    return high, low


def odd_tables(period, block):
    half = period // 2
    turn = (2 * np.arange(half)[:, None] + 1) * np.arange(period)[None, :] % (2 * period)
    phase = np.pi * turn / period
    forward = np.concatenate([np.cos(phase), -np.sin(phase)], axis=0)
    inverse = forward[:, period - block :].T / half
    return split_table(forward), split_table(inverse)


class Tables:
    def __init__(self, period, short_period, block):
        (f_high, f_low), (i_high, i_low) = odd_tables(period, block)
        (sf_high, sf_low), (si_high, si_low) = odd_tables(short_period, block)
        width = period
        self.places, rows, top = {}, [], 0
        for name, table in (("f_high", f_high), ("f_low", f_low), ("i_high", i_high), ("i_low", i_low)):
            self.places[name] = (slice(top, top + table.shape[0]), slice(0, width))
            rows.append(table)
            top += table.shape[0]
        for name, pair in (("sf", (sf_high, sf_low)), ("si", (si_high, si_low))):
            cols, height = pair[0].shape[1], pair[0].shape[0]
            self.places[name + "_high"] = (slice(top, top + height), slice(0, cols))
            self.places[name + "_low"] = (slice(top, top + height), slice(cols, 2 * cols))
            pad = np.zeros((height, width - 2 * cols), ml_dtypes.bfloat16)
            rows.append(np.concatenate([*pair, pad], axis=1))
            top += height
        self.packed = np.concatenate(rows, axis=0)

    def get(self, ref, name, first=None, last=None):
        rows, cols = self.places[name]
        start = cols.start + (first or 0)
        stop = cols.stop if last is None else cols.start + last
        return ref[rows, start:stop]


def halves(value):
    high = value.astype(BF16)
    return high, (value - high.astype(F32)).astype(BF16)


def dot(left, right):
    return jnp.dot(left, right, preferred_element_type=F32)


def wide_dot(table_high, table_low, operand):
    high, low = halves(operand)
    return dot(table_high, high) + dot(table_high, low) + dot(table_low, high)


def exact_dot(table_high, table_low, operand):
    return dot(table_high, operand) + dot(table_low, operand)


def spectra_product(first, second):
    half = first.shape[0] // 2
    a_re, a_im, b_re, b_im = first[:half], first[half:], second[:half], second[half:]
    return jnp.concatenate([a_re * b_re - a_im * b_im, a_re * b_im + a_im * b_re], axis=0)


def pieces_kernel(proj, pieces):
    width = pieces.shape[2] // 4
    for low in range(2):
        for core in range(2):
            for x in range(4):
                start = ((x * 2 + low) * 2 + core) * width
                columns = proj[:, start : start + width]
                for high in range(4):
                    pieces[(low * 4 + high) * 2 + core, :, x * width : (x + 1) * width] = columns


def lines_kernel(lines, copies, flat):
    depth = lines.shape[1]
    for source in range(lines.shape[0]):
        flat[source * depth : (source + 1) * depth, :] = lines[source].astype(F32)
    for z in range(copies.shape[0]):
        copies[z] = flat[...].astype(BF16)


def filter_kernel(tables, lags, count, both, packed, long_spec, short_spec):
    get = functools.partial(tables.get, packed)
    long_spec[...] = wide_dot(get("f_high", 0, lags), get("f_low", 0, lags), both[:lags, :])
    short_spec[...] = wide_dot(get("sf_high", 0, count), get("sf_low", 0, count), both[lags:, :])


def near_kernel(tables, third, second, first, value, packed, near, window):
    batch, rows, _ = value.shape
    get = functools.partial(tables.get, packed)
    for b in range(batch):
        for part, ref in enumerate((third, second, first, value)):
            window[part * rows : (part + 1) * rows, :] = ref[b]
        near[b] = exact_dot(get("f_high"), get("f_low"), window[...])


def mixed_kernel(tables, near, gate, spec, packed, mixed):
    batch, rows, _ = gate.shape
    channels = gate.shape[2]
    get = functools.partial(tables.get, packed)
    source = lax.broadcasted_iota(jnp.int32, (channels, channels), 0)
    column = lax.broadcasted_iota(jnp.int32, (channels, channels), 1)
    target = (lax.shift_right_logical(source, 3) & 7) * 32 + lax.shift_right_logical(source, 6) * 8
    order = (target + (source & 7) == column).astype(F32).astype(BF16)
    for b in range(batch):
        conv = wide_dot(get("i_high"), get("i_low"), spectra_product(near[b], spec[...]))
        gated = (gate[b].astype(F32) * conv).astype(BF16)
        mixed[b * rows : (b + 1) * rows, :] = dot(gated, order).astype(BF16)


def project_kernel(place, mine, over_low, over_core, over_both, plane, partial, near, far):
    core, low = place[0], place[1]
    channels, width = mine.shape[1], partial.shape[2]
    part = channels // 8
    for z in range(8):
        for target, group in ((near, low), (far, 1 - low)):
            start = pl.multiple_of((z * 2 + group) * part, part)
            target[z * part : (z + 1) * part, :] = plane[pl.ds(start, part), :]
    for here, there, block in ((mine, over_low, core), (over_core, over_both, 1 - core)):
        total = dot(here[...], near[...]) + dot(there[...], far[...])
        for x in range(partial.shape[0] // 2):
            partial[x * 2 + block] = total[:, x * width : (x + 1) * width].astype(BF16)


def sum_kernel(parts, total):
    cores, width = 2, parts.shape[2]
    for core in range(cores):
        value = parts[core].astype(F32)
        for x in range(1, parts.shape[0] // cores):
            value = value + parts[x * cores + core].astype(F32)
        total[:, core * width : (core + 1) * width] = value.astype(BF16)


def own_kernel(tables, own, packed, near):
    rows = own.shape[0] // near.shape[0]
    skipped = near.shape[1] - rows
    get = functools.partial(tables.get, packed)
    for b in range(near.shape[0]):
        block = own[b * rows : (b + 1) * rows, :]
        near[b] = exact_dot(get("sf_high", skipped), get("sf_low", skipped), block)


def output_kernel(tables, rim, near, gate, spec, packed, result):
    batch, rows, _ = gate.shape
    skipped = near.shape[1] - rows
    get = functools.partial(tables.get, packed)
    for b in range(batch):
        block = rim[b * rows : (b + 1) * rows, :]
        spectrum = near[b] + exact_dot(get("sf_high", 0, skipped), get("sf_low", 0, skipped), block)
        shorted = wide_dot(get("si_high"), get("si_low"), spectra_product(spectrum, spec[...]))
        result[b] = (gate[b].astype(F32) * shorted).astype(BF16)


def call(kernel, outs, flops, scratch=(), left=(), grant=20):
    def run(*args):
        many = isinstance(outs, (list, tuple))
        specs = [HBM if i in left else SMEM if a.dtype == jnp.int32 else VMEM for i, a in enumerate(args)]
        size = sum(a.size * a.dtype.itemsize for a in args)
        return pl.pallas_call(
            kernel,
            out_shape=outs,
            in_specs=specs,
            out_specs=[VMEM] * len(outs) if many else VMEM,
            scratch_shapes=list(scratch),
            compiler_params=pltpu.CompilerParams(vmem_limit_bytes=grant * 1024 * 1024),
            cost_estimate=pl.CostEstimate(flops=flops, bytes_accessed=size, transcendentals=0),
        )(*args)

    return run


def from_behind(value, steps):
    count = lax.axis_size("ctx")
    return lax.ppermute(value, "ctx", [(s, s + steps) for s in range(count - steps)])


def shape(dims, dtype):
    return jax.ShapeDtypeStruct(dims, dtype)


def after(value, *earlier):
    return lax.optimization_barrier((value,) + earlier)[0]


def per_device(value, gate_in, gate_out, filters, skip, proj, taps):
    batch, rows, channels = value.shape
    lags, count = filters.shape[0], taps.shape[0]
    period, short_period = lags + rows, count + rows
    tables = Tables(period, short_period, rows)
    packed = jnp.asarray(tables.packed)
    place = jnp.stack([lax.axis_index("ctx") % 2, lax.axis_index("chan") % 2]).astype(jnp.int32)
    depth, width = proj.shape
    wide = batch * rows
    part = channels // 2

    def device(x, low, high, z, core):
        return (x * 2 + low) * 64 + high * 16 + z * 2 + core

    def exchange(pieces, groups):
        return lax.all_to_all(
            pieces, ("chan", "ctx"), 0, 0, axis_index_groups=groups, tiled=True
        )

    xs, lows, highs, zs, cores = range(4), range(2), range(4), range(8), range(2)
    along_y = [
        [device(x, low, high, z, c) for low in lows for high in highs for c in cores]
        for x in xs for z in zs
    ]
    along_z = [
        [device(x, low, high, z, c) for z in zs]
        for x in xs for low in lows for high in highs for c in cores
    ]
    along_x = [
        [device(x, low, high, z, c) for x in xs for c in cores]
        for low in lows for high in highs for z in zs
    ]

    pieces = call(pieces_kernel, shape((16, depth, width // 4), BF16), 1000)(proj)
    lines = exchange(pieces, along_y)
    moved = after(value, pieces)
    first = from_behind(moved, 1)
    second = from_behind(moved, 2)
    both = jnp.concatenate([filters[:1] + skip[None], filters[1:], taps], axis=0)
    spec, short_spec = call(
        functools.partial(filter_kernel, tables, lags, count),
        (shape((period, channels), F32), shape((short_period, channels), F32)),
        6 * period * lags * channels,
    )(both, packed)
    third = from_behind(moved, 3)
    near = call(
        functools.partial(near_kernel, tables),
        shape((batch, period, channels), F32),
        40 * batch * 2 * period * lags * channels,
        [pltpu.VMEM((period, channels), BF16)],
    )(third, second, first, value, packed)
    lines = call(
        lines_kernel,
        shape((8, 16 * depth, width // 4), BF16),
        1000,
        [pltpu.VMEM((16 * depth, width // 4), F32)],
    )(lines)
    plane = exchange(lines, along_z).reshape(8 * 16 * depth, width // 4)
    mixed = call(
        functools.partial(mixed_kernel, tables),
        shape((wide, channels), BF16),
        20 * batch * 2 * period * rows * channels * 5,
    )(near, gate_in, spec, packed)

    def across(flip):
        pairs = [(d, d ^ flip) for d in range(lax.axis_size("chan") * lax.axis_size("ctx"))]
        return lax.ppermute(mixed, ("chan", "ctx"), pairs)

    over_low, over_core, over_both = across(64), across(1), across(65)
    partial = call(
        project_kernel,
        shape((8, wide, part), BF16),
        2 * wide * 2 * channels * width,
        [pltpu.VMEM((channels, width // 4), BF16)] * 2,
    )(place, mixed, over_low, over_core, over_both, plane)
    parts = exchange(partial, along_x)
    projected = call(sum_kernel, shape((wide, channels), BF16), wide * channels * 4)(parts)
    rim = from_behind(projected, 1)
    near = call(
        functools.partial(own_kernel, tables),
        shape((batch, short_period, channels), F32),
        2 * batch * 2 * short_period * rows * channels,
    )(projected, packed)
    return call(
        functools.partial(output_kernel, tables),
        shape((batch, rows, channels), BF16),
        batch * 2 * short_period * rows * channels * 5,
    )(rim, near, gate_out, short_spec, packed)


def solution(mesh):
    in_specs = (
        P(None, "ctx", "chan"),
        P(None, "ctx", "chan"),
        P(None, "ctx", "chan"),
        P(None, "chan"),
        P("chan"),
        P(("chan", "ctx"), None),
        P(None, "chan"),
    )
    out_specs = P(None, "ctx", "chan")
    return jax.shard_map(
        per_device, mesh=mesh, in_specs=in_specs, out_specs=out_specs, check_vma=False
    )
```

```python
import functools

import jax
import jax.numpy as jnp
import ml_dtypes
import numpy as np
from jax import lax
from jax.experimental import pallas as pl
from jax.experimental.pallas import tpu as pltpu
from jax.sharding import PartitionSpec as P

F32 = jnp.float32
BF16 = jnp.bfloat16
VMEM = pl.BlockSpec(memory_space=pltpu.VMEM)
SMEM = pl.BlockSpec(memory_space=pltpu.SMEM)
HBM = pl.BlockSpec(memory_space=pltpu.HBM)


def split_table(table):
    high = table.astype(ml_dtypes.bfloat16)
    low = (table - high.astype(np.float64)).astype(ml_dtypes.bfloat16)
    return high, low


def odd_tables(period, block):
    half = period // 2
    turn = (2 * np.arange(half)[:, None] + 1) * np.arange(period)[None, :] % (2 * period)
    phase = np.pi * turn / period
    forward = np.concatenate([np.cos(phase), -np.sin(phase)], axis=0)
    inverse = forward[:, period - block :].T / half
    return split_table(forward), split_table(inverse)


class Tables:
    def __init__(self, period, short_period, block):
        (f_high, f_low), (i_high, i_low) = odd_tables(period, block)
        (sf_high, sf_low), (si_high, si_low) = odd_tables(short_period, block)
        width = period
        self.places, rows, top = {}, [], 0
        for name, table in (("f_high", f_high), ("f_low", f_low), ("i_high", i_high), ("i_low", i_low)):
            self.places[name] = (slice(top, top + table.shape[0]), slice(0, width))
            rows.append(table)
            top += table.shape[0]
        for name, pair in (("sf", (sf_high, sf_low)), ("si", (si_high, si_low))):
            cols, height = pair[0].shape[1], pair[0].shape[0]
            self.places[name + "_high"] = (slice(top, top + height), slice(0, cols))
            self.places[name + "_low"] = (slice(top, top + height), slice(cols, 2 * cols))
            pad = np.zeros((height, width - 2 * cols), ml_dtypes.bfloat16)
            rows.append(np.concatenate([*pair, pad], axis=1))
            top += height
        self.packed = np.concatenate(rows, axis=0)

    def get(self, ref, name, first=None, last=None):
        rows, cols = self.places[name]
        start = cols.start + (first or 0)
        stop = cols.stop if last is None else cols.start + last
        return ref[rows, start:stop]


def halves(value):
    high = value.astype(BF16)
    return high, (value - high.astype(F32)).astype(BF16)


def dot(left, right):
    return jnp.dot(left, right, preferred_element_type=F32)


def wide_dot(table_high, table_low, operand):
    high, low = halves(operand)
    return dot(table_high, high) + dot(table_high, low) + dot(table_low, high)


def exact_dot(table_high, table_low, operand):
    return dot(table_high, operand) + dot(table_low, operand)


def spectra_product(first, second):
    half = first.shape[0] // 2
    a_re, a_im, b_re, b_im = first[:half], first[half:], second[:half], second[half:]
    return jnp.concatenate([a_re * b_re - a_im * b_im, a_re * b_im + a_im * b_re], axis=0)


def pieces_kernel(proj, pieces):
    width = pieces.shape[2] // 4
    for low in range(2):
        for core in range(2):
            for x in range(4):
                start = ((x * 2 + low) * 2 + core) * width
                columns = proj[:, start : start + width]
                for high in range(4):
                    pieces[(low * 4 + high) * 2 + core, :, x * width : (x + 1) * width] = columns


def lines_kernel(lines, copies, flat):
    depth = lines.shape[1]
    for source in range(lines.shape[0]):
        flat[source * depth : (source + 1) * depth, :] = lines[source].astype(F32)
    for z in range(copies.shape[0]):
        copies[z] = flat[...].astype(BF16)


def filter_kernel(tables, lags, count, both, packed, long_spec, short_spec):
    get = functools.partial(tables.get, packed)
    long_spec[...] = wide_dot(get("f_high", 0, lags), get("f_low", 0, lags), both[:lags, :])
    short_spec[...] = wide_dot(get("sf_high", 0, count), get("sf_low", 0, count), both[lags:, :])


def near_kernel(tables, third, second, first, value, packed, near, window):
    batch, rows, _ = value.shape
    get = functools.partial(tables.get, packed)
    for b in range(batch):
        for part, ref in enumerate((third, second, first, value)):
            window[part * rows : (part + 1) * rows, :] = ref[b]
        near[b] = exact_dot(get("f_high"), get("f_low"), window[...])


def mixed_kernel(tables, near, gate, spec, packed, mixed):
    batch, rows, _ = gate.shape
    channels = gate.shape[2]
    get = functools.partial(tables.get, packed)
    source = lax.broadcasted_iota(jnp.int32, (channels, channels), 0)
    column = lax.broadcasted_iota(jnp.int32, (channels, channels), 1)
    target = (lax.shift_right_logical(source, 3) & 7) * 32 + lax.shift_right_logical(source, 6) * 8
    order = (target + (source & 7) == column).astype(F32).astype(BF16)
    for b in range(batch):
        conv = wide_dot(get("i_high"), get("i_low"), spectra_product(near[b], spec[...]))
        gated = (gate[b].astype(F32) * conv).astype(BF16)
        mixed[b * rows : (b + 1) * rows, :] = dot(gated, order).astype(BF16)


def project_kernel(place, mine, over_low, over_core, over_both, plane, partial, near, far):
    core, low = place[0], place[1]
    channels, width = mine.shape[1], partial.shape[2]
    part = channels // 8
    for z in range(8):
        for target, group in ((near, low), (far, 1 - low)):
            start = pl.multiple_of((z * 2 + group) * part, part)
            target[z * part : (z + 1) * part, :] = plane[pl.ds(start, part), :]
    for here, there, block in ((mine, over_low, core), (over_core, over_both, 1 - core)):
        total = dot(here[...], near[...]) + dot(there[...], far[...])
        for x in range(partial.shape[0] // 2):
            partial[x * 2 + block] = total[:, x * width : (x + 1) * width].astype(BF16)


def sum_kernel(parts, total):
    cores, width = 2, parts.shape[2]
    for core in range(cores):
        value = parts[core].astype(F32)
        for x in range(1, parts.shape[0] // cores):
            value = value + parts[x * cores + core].astype(F32)
        total[:, core * width : (core + 1) * width] = value.astype(BF16)


def own_kernel(tables, own, packed, near):
    rows = own.shape[0] // near.shape[0]
    skipped = near.shape[1] - rows
    get = functools.partial(tables.get, packed)
    for b in range(near.shape[0]):
        block = own[b * rows : (b + 1) * rows, :]
        near[b] = exact_dot(get("sf_high", skipped), get("sf_low", skipped), block)


def output_kernel(tables, rim, near, gate, spec, packed, result):
    batch, rows, _ = gate.shape
    skipped = near.shape[1] - rows
    get = functools.partial(tables.get, packed)
    for b in range(batch):
        block = rim[b * rows : (b + 1) * rows, :]
        spectrum = near[b] + exact_dot(get("sf_high", 0, skipped), get("sf_low", 0, skipped), block)
        shorted = wide_dot(get("si_high"), get("si_low"), spectra_product(spectrum, spec[...]))
        result[b] = (gate[b].astype(F32) * shorted).astype(BF16)


def call(kernel, outs, flops, scratch=(), left=(), grant=20):
    def run(*args):
        many = isinstance(outs, (list, tuple))
        specs = [HBM if i in left else SMEM if a.dtype == jnp.int32 else VMEM for i, a in enumerate(args)]
        size = sum(a.size * a.dtype.itemsize for a in args)
        return pl.pallas_call(
            kernel,
            out_shape=outs,
            in_specs=specs,
            out_specs=[VMEM] * len(outs) if many else VMEM,
            scratch_shapes=list(scratch),
            compiler_params=pltpu.CompilerParams(vmem_limit_bytes=grant * 1024 * 1024),
            cost_estimate=pl.CostEstimate(flops=flops, bytes_accessed=size, transcendentals=0),
        )(*args)

    return run


def from_behind(value, steps):
    count = lax.axis_size("ctx")
    return lax.ppermute(value, "ctx", [(s, s + steps) for s in range(count - steps)])


def shape(dims, dtype):
    return jax.ShapeDtypeStruct(dims, dtype)


def after(value, *earlier):
    return lax.optimization_barrier((value,) + earlier)[0]


def per_device(value, gate_in, gate_out, filters, skip, proj, taps):
    batch, rows, channels = value.shape
    lags, count = filters.shape[0], taps.shape[0]
    period, short_period = lags + rows, count + rows
    tables = Tables(period, short_period, rows)
    packed = jnp.asarray(tables.packed)
    place = jnp.stack([lax.axis_index("ctx") % 2, lax.axis_index("chan") % 2]).astype(jnp.int32)
    depth, width = proj.shape
    wide = batch * rows
    part = channels // 2

    def device(x, low, high, z, core):
        return (x * 2 + low) * 64 + high * 16 + z * 2 + core

    def exchange(pieces, groups):
        return lax.all_to_all(
            pieces, ("chan", "ctx"), 0, 0, axis_index_groups=groups, tiled=True
        )

    xs, lows, highs, zs, cores = range(4), range(2), range(4), range(8), range(2)
    along_y = [
        [device(x, low, high, z, c) for low in lows for high in highs for c in cores]
        for x in xs for z in zs
    ]
    along_z = [
        [device(x, low, high, z, c) for z in zs]
        for x in xs for low in lows for high in highs for c in cores
    ]
    along_x = [
        [device(x, low, high, z, c) for x in xs for c in cores]
        for low in lows for high in highs for z in zs
    ]

    pieces = call(pieces_kernel, shape((16, depth, width // 4), BF16), 1000)(proj)
    lines = exchange(pieces, along_y)
    moved = after(value, pieces)
    first = from_behind(moved, 1)
    second = from_behind(moved, 2)
    both = jnp.concatenate([filters[:1] + skip[None], filters[1:], taps], axis=0)
    spec, short_spec = call(
        functools.partial(filter_kernel, tables, lags, count),
        (shape((period, channels), F32), shape((short_period, channels), F32)),
        6 * period * lags * channels,
    )(both, packed)
    third = from_behind(moved, 3)
    near = call(
        functools.partial(near_kernel, tables),
        shape((batch, period, channels), F32),
        16 * batch * 2 * period * lags * channels,
        [pltpu.VMEM((period, channels), BF16)],
    )(third, second, first, value, packed)
    lines = call(
        lines_kernel,
        shape((8, 16 * depth, width // 4), BF16),
        1000,
        [pltpu.VMEM((16 * depth, width // 4), F32)],
    )(lines)
    plane = exchange(lines, along_z).reshape(8 * 16 * depth, width // 4)
    mixed = call(
        functools.partial(mixed_kernel, tables),
        shape((wide, channels), BF16),
        8 * batch * 2 * period * rows * channels * 5,
    )(near, gate_in, spec, packed)

    def across(flip):
        pairs = [(d, d ^ flip) for d in range(lax.axis_size("chan") * lax.axis_size("ctx"))]
        return lax.ppermute(mixed, ("chan", "ctx"), pairs)

    over_low, over_core, over_both = across(64), across(1), across(65)
    partial = call(
        project_kernel,
        shape((8, wide, part), BF16),
        2 * wide * 2 * channels * width,
        [pltpu.VMEM((channels, width // 4), BF16)] * 2,
    )(place, mixed, over_low, over_core, over_both, plane)
    parts = exchange(partial, along_x)
    projected = call(sum_kernel, shape((wide, channels), BF16), wide * channels * 4)(parts)
    rim = from_behind(projected, 1)
    near = call(
        functools.partial(own_kernel, tables),
        shape((batch, short_period, channels), F32),
        2 * batch * 2 * short_period * rows * channels,
    )(projected, packed)
    return call(
        functools.partial(output_kernel, tables),
        shape((batch, rows, channels), BF16),
        batch * 2 * short_period * rows * channels * 5,
    )(rim, near, gate_out, short_spec, packed)


def solution(mesh):
    in_specs = (
        P(None, "ctx", "chan"),
        P(None, "ctx", "chan"),
        P(None, "ctx", "chan"),
        P(None, "chan"),
        P("chan"),
        P(("chan", "ctx"), None),
        P(None, "chan"),
    )
    out_specs = P(None, "ctx", "chan")
    return jax.shard_map(
        per_device, mesh=mesh, in_specs=in_specs, out_specs=out_specs, check_vma=False
    )
```
